32 devices in a mesh: row: 4 (over y, x), col: 8 (over z, core).
Axes of the slice: x: 2, y: 2, z: 4, core: 2. Of those that a mesh axis runs over, the one named last changes fastest.
Arguments:
- inverse_sep: float32 [12288, 12288], P('row', 'col'), may hold values from -105 to 105, as said below
- sep_panels: float32 [3, 12288, 256], P(None, 'row', 'col'), may hold values from -0.0546875 to 0.0546875
- chain_panels: float32 [3, 256, 256], P(None, 'row', 'col'), may hold values from -0.375 to 0.375
- diag_inverse: float32 [3, 256, 256], P(None, 'row'), may hold values from -5 to 5, as said below
- tile_list: int32 [3, 96], replicated, may hold values from 0 to 1, as said below
Outputs:
- sep_rows: float32 [3, 256, 12288], P(None, 'row', 'col')
- chain_inverse: float32 [3, 256, 768], P(None, 'row')
The draws below stay inside these ranges and needn't reach their ends.
Inputs may be any that keep to these rules, and one draw needn't show every extreme that they name: `inverse_sep`: symmetric. `diag_inverse`: each block symmetric. `tile_list`: a tile listed for supernode k is listed for every earlier supernode.
All inputs are finite; a program needn't handle non-finite values.
Results may differ from the reference program's by a relative error of at most 0.00013.
Values sent between devices are 32-bit elements; how exact they have to be, the bound alone decides.
A program may use at most 128 MiB of HBM per device.

```python
import jax
import jax.numpy as jnp
from jax import lax

NS = 12288
NB = 256
TILE = 128
NSUPER = 3
NPAIR = 3
NTILE = 96


def draw_inverse_sep(key, part):
    key_noise, key_diag = jax.random.split(jax.random.fold_in(key, 101), 2)
    noise = jnp.clip(jax.random.normal(key_noise, (NS, NS), jnp.float32), -7.0, 7.0)
    values_sym = (noise + noise.T) * 0.7071
    diag_index = jnp.arange(NS)
    return values_sym.at[diag_index, diag_index].add(jax.random.uniform(key_diag, (NS,), jnp.float32, 1.0, 4.0))


def draw_diag_inverse(key, part):
    key_noise, key_diag = jax.random.split(jax.random.fold_in(key, 202), 2)
    noise = jnp.clip(jax.random.normal(key_noise, (NSUPER, NB, NB), jnp.float32), -6.0, 6.0)
    blocks = (noise + jnp.swapaxes(noise, 1, 2)) * (0.5 / NB ** 0.5)
    diagonal = jax.random.uniform(key_diag, (NSUPER, NB), jnp.float32, 0.5, 2.0)
    return blocks + jnp.eye(NB, dtype=jnp.float32)[None] * diagonal[:, None, :]


def draw_tile_list(key, part):
    levels = jax.random.randint(jax.random.fold_in(key, 303), (NSUPER, NTILE), 0, 4)
    present = (levels > 0).astype(jnp.int32)
    return jnp.cumprod(present, axis=0).astype(jnp.int32)


def steps_of(rng, dims, pieces, least, top_value):
    loudness, own = 1.0, jax.random.fold_in(rng, 6)
    for axis_at, shards_of in pieces:
        heights = jnp.exp(jax.random.uniform(jax.random.fold_in(own, axis_at), (shards_of,), jnp.float32, least / len(pieces), top_value / len(pieces)))
        loudness = loudness * jnp.repeat(heights, dims[axis_at] // shards_of).reshape([-1 if axis == axis_at else 1 for axis in range(len(dims))])
    return loudness


def normal_values(stream_key, extent, scale, limit, pieces=(), kind=jnp.bfloat16):
    values = scale * jax.random.normal(stream_key, extent, jnp.float32)
    if pieces:
        values = values * steps_of(stream_key, extent, pieces, -0.22, 0.18)
    return jnp.clip(values, -limit, limit).astype(kind)


def setup_inputs(seed: int = 0) -> dict:
    streams_of = jax.random.split(jax.random.key(seed), 6)
    inverse_sep = draw_inverse_sep(jax.random.fold_in(streams_of[5], 71), 0)
    sep_panels = normal_values(streams_of[1], (NSUPER, NS, NB), NS ** -0.5, 0.0546875, ((1, 4), (2, 8)), jnp.float32)
    chain_panels = normal_values(streams_of[2], (NPAIR, NB, NB), NB ** -0.5, 0.375, ((1, 4), (2, 8)), jnp.float32)
    diag_inverse = draw_diag_inverse(jax.random.fold_in(streams_of[5], 71), 0)
    tile_list = draw_tile_list(jax.random.fold_in(streams_of[5], 71), 0)
    return dict(inverse_sep=inverse_sep, sep_panels=sep_panels, chain_panels=chain_panels, diag_inverse=diag_inverse, tile_list=tile_list)


def pair_index(current, earlier):
    return current * (current - 1) // 2 + earlier


def product(left, right):
    return jnp.dot(left, right, precision=lax.Precision.HIGHEST, preferred_element_type=jnp.float32)


def inner_product(left, right):
    return lax.dot_general(left, right, (((0,), (0,)), ((), ())), precision=lax.Precision.HIGHEST, preferred_element_type=jnp.float32)


def reference(inverse_sep, sep_panels, chain_panels, diag_inverse, tile_list):
    chain_state = jnp.zeros((NSUPER, NB, NSUPER * NB), jnp.float32)
    new_rows = []
    for current in range(NSUPER):
        listed = jnp.repeat(tile_list[current].astype(jnp.float32), TILE)
        panel = sep_panels[current] * listed[:, None]
        summed = inner_product(panel, inverse_sep)
        for earlier in range(current):
            summed = summed + inner_product(chain_panels[pair_index(current, earlier)], new_rows[earlier])
        rows_now = -summed
        first_term = product(rows_now, panel)
        crossing = []
        for earlier in range(current):
            crossed = product(new_rows[earlier], panel)
            for middle in range(current):
                crossed = crossed + product(chain_state[earlier, :, middle * NB:(middle + 1) * NB], chain_panels[pair_index(current, middle)])
            crossing.append(-crossed)
        second_term = jnp.zeros((NB, NB), jnp.float32)
        for earlier in range(current):
            chain_state = chain_state.at[earlier, :, current * NB:(current + 1) * NB].set(crossing[earlier])
            chain_state = chain_state.at[current, :, earlier * NB:(earlier + 1) * NB].set(crossing[earlier].T)
            second_term = second_term + product(crossing[earlier].T, chain_panels[pair_index(current, earlier)])
        chain_state = chain_state.at[current, :, current * NB:(current + 1) * NB].set(diag_inverse[current] - first_term - second_term)
        new_rows.append(rows_now)
    return jnp.stack(new_rows), chain_state
```

```python
import jax
import jax.numpy as jnp
from jax import lax
from jax.sharding import PartitionSpec as P

NB = 256
TILE = 128
NSUPER = 3


def pair_index(current, earlier):
    return current * (current - 1) // 2 + earlier


def dot(left, right, left_dim, right_dim, precision=lax.Precision.HIGH):
    return lax.dot_general(
        left,
        right,
        (((left_dim,), (right_dim,)), ((), ())),
        precision=precision,
        preferred_element_type=jnp.float32,
    )


def finish(total, chain, diag):
    highest = lax.Precision.HIGHEST
    blocks = {}
    for current in range(NSUPER):
        crossing = []
        for earlier in range(current):
            crossed = total[earlier, current]
            for middle in range(current):
                crossed = crossed + dot(
                    blocks[earlier, middle], chain[pair_index(current, middle)], 1, 0, highest
                )
            crossing.append(-crossed)
        own = diag[current] - total[current, current]
        for earlier in range(current):
            blocks[earlier, current] = crossing[earlier]
            blocks[current, earlier] = crossing[earlier].T
            own = own - dot(
                crossing[earlier], chain[pair_index(current, earlier)], 0, 0, highest
            )
        blocks[current, current] = own
    return jnp.stack(
        [
            jnp.concatenate([blocks[line, column] for column in range(NSUPER)], axis=1)
            for line in range(NSUPER)
        ]
    )


def per_device(inverse_sep, sep_panels, chain_panels, diag_inverse, tile_list):
    row_count = lax.axis_size("row")
    col_count = lax.axis_size("col")
    row_place = lax.axis_index("row")
    col_place = lax.axis_index("col")
    row_cells, col_cells = inverse_sep.shape
    nb_rows = NB // row_count
    nb_cols = NB // col_count
    ratio_cols = col_count // row_count
    root_row = col_place // ratio_cols
    inner_part = col_place % ratio_cols
    tile_rows = row_cells // TILE
    listed = lax.dynamic_slice_in_dim(tile_list, row_place * tile_rows, tile_rows, 1)
    listed = jnp.repeat(listed.astype(jnp.float32), TILE, axis=1)

    local = jnp.swapaxes(sep_panels, 1, 2) * listed[:, None, :]
    panels = [
        lax.all_gather(local[current], "col", axis=0, tiled=True) for current in range(NSUPER)
    ]
    diag_part = lax.dynamic_slice_in_dim(diag_inverse, col_place * nb_cols, nb_cols, 2)
    small = jnp.stack([chain_panels, diag_part]).reshape(-1, 128)
    small = lax.all_gather(small, ("row", "col"), axis=0, tiled=False)
    small = small.reshape(row_count, col_count, 2, NSUPER, nb_rows, nb_cols)
    small = small.transpose(2, 3, 0, 4, 1, 5).reshape(2, NSUPER, NB, NB)
    chain, diag = small[0], small[1]

    is_root = row_place == root_row
    partial = []
    rows = []
    total = {}
    for current in range(NSUPER):
        summed = -dot(panels[current], inverse_sep, 1, 0)
        for earlier in range(current):
            summed = summed - dot(chain[pair_index(current, earlier)], partial[earlier], 0, 0)
        partial.append(summed)
        if rows:
            summed, rows[-1] = lax.optimization_barrier((summed, rows[-1]))
        rows.append(lax.psum(summed, "row"))
        own_panel = lax.dynamic_slice_in_dim(panels[current], inner_part * col_cells, col_cells, 1)
        for earlier in range(current + 1):
            total[earlier, current] = dot(rows[earlier], own_panel, 1, 1)
    keys = sorted(total)
    stacked = jnp.stack([total[key] for key in keys])
    stacked = lax.psum(jnp.where(is_root, stacked, 0.0), ("row", "col"))
    total = {key: stacked[place] for place, key in enumerate(keys)}
    state = finish(total, chain, diag)
    state = lax.dynamic_slice_in_dim(state, row_place * nb_rows, nb_rows, 1)
    new_rows = jnp.stack(
        [lax.dynamic_slice_in_dim(row, row_place * nb_rows, nb_rows, 0) for row in rows]
    )
    return new_rows, state


def solution(mesh):
    in_specs = (
        P("row", "col"),
        P(None, "row", "col"),
        P(None, "row", "col"),
        P(None, "row", None),
        P(),
    )
    out_specs = (P(None, "row", "col"), P(None, "row", None))
    return jax.shard_map(
        per_device, mesh=mesh, in_specs=in_specs, out_specs=out_specs, check_vma=False
    )
```

```python
import functools

import jax
import jax.numpy as jnp
from jax import lax
from jax.experimental import pallas as pl
from jax.experimental.pallas import tpu as pltpu
from jax.sharding import PartitionSpec as P

NB = 256
TILE = 128
NSUPER = 3
VMEM = pl.BlockSpec(memory_space=pltpu.VMEM)
VMEM_BYTES = 40 * 1024 * 1024


def pair_index(current, earlier):
    return current * (current - 1) // 2 + earlier


def total_index(earlier, current):
    return current * (current + 1) // 2 + earlier


def dot(left, right, left_dim, right_dim, precision=lax.Precision.HIGH):
    return lax.dot_general(
        left,
        right,
        (((left_dim,), (right_dim,)), ((), ())),
        precision=precision,
        preferred_element_type=jnp.float32,
    )


def send(source, target, sems, place, device):
    return pltpu.make_async_remote_copy(
        src_ref=source,
        dst_ref=target,
        send_sem=sems[0].at[place],
        recv_sem=sems[1].at[place],
        device_id=device,
        device_id_type=pl.DeviceIdType.MESH,
    )


def signal(device):
    pl.semaphore_signal(
        pltpu.get_barrier_semaphore(),
        inc=1,
        device_id=device,
        device_id_type=pl.DeviceIdType.MESH,
    )


def communicating(kernel, collective_id, out_shape, scratch_shapes, inputs):
    return pl.pallas_call(
        kernel,
        out_shape=out_shape,
        in_specs=[VMEM] * len(inputs),
        out_specs=jax.tree.map(lambda _: VMEM, out_shape),
        scratch_shapes=scratch_shapes,
        compiler_params=pltpu.CompilerParams(
            collective_id=collective_id, has_side_effects=True, vmem_limit_bytes=VMEM_BYTES
        ),
    )(*inputs)


def sem_pair(count):
    return [pltpu.SemaphoreType.DMA((count,)), pltpu.SemaphoreType.DMA((count,))]


def gather_kernel(
    row_count, col_count, chain, diag, all_chain, all_diag, s0, r0, s1, r1, s2, r2
):
    me_row, me_col = lax.axis_index("row"), lax.axis_index("col")
    for step in range(1, col_count):
        signal((me_row, lax.rem(me_col + step, col_count)))
    for step in range(1, row_count):
        signal((lax.rem(me_row + step, row_count), me_col))
    pl.semaphore_wait(pltpu.get_barrier_semaphore(), row_count + col_count - 2)
    copies = []
    for step in range(1, col_count):
        device = (me_row, lax.rem(me_col + step, col_count))
        copies.append(send(chain, all_chain.at[me_row, me_col], (s0, r0), step, device))
    later = []
    for step in range(1, row_count):
        device = (lax.rem(me_row + step, row_count), me_col)
        later.append(send(diag, all_diag.at[me_row], (s1, r1), step, device))
    for copy in copies + later:
        copy.start()
    all_chain[me_row, me_col] = chain[...]
    all_diag[me_row] = diag[...]
    for copy in copies:
        copy.wait()
    rows = []
    for step in range(1, row_count):
        device = (lax.rem(me_row + step, row_count), me_col)
        rows.append(send(all_chain.at[me_row], all_chain.at[me_row], (s2, r2), step, device))
    for copy in rows:
        copy.start()
    for copy in later + rows:
        copy.wait()


def row_sum_kernel(row_count, ratio, part, own, full, landed, s0, r0, s1, r1):
    me_row, me_col = lax.axis_index("row"), lax.axis_index("col")
    cells = own.shape[0]
    root = me_col // ratio

    def rows_of(place):
        return pl.ds(pl.multiple_of(place * cells, cells), cells)

    for step in range(1, row_count):
        signal((lax.rem(me_row + step, row_count), me_col))
    pl.semaphore_wait(pltpu.get_barrier_semaphore(), row_count - 1)
    copies = []
    for step in range(1, row_count):
        peer = lax.rem(me_row + step, row_count)
        copies.append(
            send(part.at[rows_of(peer)], landed.at[step], (s0, r0), step, (peer, me_col))
        )
    for copy in copies:
        copy.start()
    total = part[rows_of(me_row), :]
    for step, copy in enumerate(copies):
        copy.wait_recv()
        total = total + landed[step + 1]
    own[...] = total

    for step in range(1, row_count):
        peer = lax.rem(me_row + step, row_count)

        @pl.when(peer == root)
        def _():
            copy = send(own, full.at[rows_of(me_row)], (s1, r1), step, (peer, me_col))
            copy.start()
            copy.wait_send()

    @pl.when(me_row == root)
    def _():
        full[rows_of(me_row), :] = own[...]
        for step in range(1, row_count):
            peer = lax.rem(me_row + row_count - step, row_count)
            send(own, full.at[rows_of(peer)], (s1, r1), step, (peer, me_col)).wait_recv()

    for copy in copies:
        copy.wait_send()


def total_kernel(
    row_count, col_count, ratio, part, full, landed, s0, r0, s1, r1, s2, r2, s3, r3
):
    me_row, me_col = lax.axis_index("row"), lax.axis_index("col")
    cells = part.shape[0] // col_count
    half = col_count // 2
    root = me_col // ratio
    sibling = me_col + 1 - 2 * lax.rem(me_col, 2)

    def rows_of(place):
        return pl.ds(pl.multiple_of(place * cells, cells), cells)

    mine = full.at[rows_of(me_col)]
    for step in range(1, row_count):
        signal((lax.rem(me_row + step, row_count), me_col))
    for step in range(1, col_count):
        signal((me_row, lax.rem(me_col + step, col_count)))

    @pl.when(me_row != root)
    def _():
        pl.semaphore_wait(pltpu.get_barrier_semaphore(), row_count + col_count - 2)

    @pl.when(me_row == root)
    def _():
        for step in range(1, col_count):
            peer = lax.rem(me_col + step, col_count)
            signal((peer // ratio, peer))
        pl.semaphore_wait(pltpu.get_barrier_semaphore(), row_count + 2 * col_count - 3)
        copies = []
        for step in range(1, col_count):
            peer = lax.rem(me_col + step, col_count)
            copies.append(
                send(part.at[rows_of(peer)], landed.at[step], (s0, r0), step, (peer // ratio, peer))
            )
        for copy in copies:
            copy.start()
        total = part[rows_of(me_col), :]
        for step, copy in enumerate(copies):
            copy.wait_recv()
            total = total + landed[step + 1]
        full[rows_of(me_col), :] = total
        downs = []
        for step in range(1, row_count):
            device = (lax.rem(me_row + step, row_count), me_col)
            downs.append(send(mine, mine, (s1, r1), step, device))
        for copy in downs:
            copy.start()
        for copy in copies + downs:
            copy.wait_send()

    for step in range(1, row_count):
        peer = lax.rem(me_row + row_count - step, row_count)

        @pl.when(peer == root)
        def _():
            send(mine, mine, (s1, r1), step, (peer, me_col)).wait_recv()

    across = []
    for step in range(1, half):
        device = (me_row, lax.rem(me_col + 2 * step, col_count))
        across.append(send(mine, mine, (s2, r2), step, device))
    for copy in across:
        copy.start()
    beside = []
    for step in range(half):
        if step:
            across[step - 1].wait_recv()
        held = lax.rem(me_col + col_count - 2 * step, col_count)
        block = full.at[rows_of(held)]
        beside.append(send(block, block, (s3, r3), step, (me_row, sibling)))
        beside[-1].start()
    for copy in across:
        copy.wait_send()
    for copy in beside:
        copy.wait()


def finish_kernel(total, chain, diag, state):
    highest = lax.Precision.HIGHEST
    blocks = {}

    def total_of(earlier, current):
        return total[total_index(earlier, current) * NB : (total_index(earlier, current) + 1) * NB]

    for current in range(NSUPER):
        crossing = []
        for earlier in range(current):
            crossed = total_of(earlier, current)
            for middle in range(current):
                crossed = crossed + dot(
                    blocks[earlier, middle], chain[pair_index(current, middle)], 1, 0, highest
                )
            crossing.append(-crossed)
        own = diag[current] - total_of(current, current)
        for earlier in range(current):
            blocks[earlier, current] = crossing[earlier]
            blocks[current, earlier] = crossing[earlier].T
            own = own - dot(
                blocks[current, earlier], chain[pair_index(current, earlier)], 1, 0, highest
            )
        blocks[current, current] = own
    for line in range(NSUPER):
        for column in range(NSUPER):
            state[line, :, column * NB : (column + 1) * NB] = blocks[line, column]


def per_device(inverse_sep, sep_panels, chain_panels, diag_inverse, tile_list):
    row_count = lax.axis_size("row")
    col_count = lax.axis_size("col")
    row_place = lax.axis_index("row")
    col_place = lax.axis_index("col")
    row_cells, col_cells = inverse_sep.shape
    nb_rows = NB // row_count
    nb_cols = NB // col_count
    ratio_cols = col_count // row_count
    inner_part = col_place % ratio_cols
    tile_rows = row_cells // TILE
    listed = lax.dynamic_slice_in_dim(tile_list, row_place * tile_rows, tile_rows, 1)
    listed = jnp.repeat(listed.astype(jnp.float32), TILE, axis=1)

    local = jnp.swapaxes(sep_panels, 1, 2) * listed[:, None, :]
    panels = [
        lax.all_gather(local[current], "col", axis=0, tiled=True) for current in range(NSUPER)
    ]
    packed = chain_panels.reshape(-1, TILE)
    all_chain, all_diag = communicating(
        functools.partial(gather_kernel, row_count, col_count),
        0,
        (
            jax.ShapeDtypeStruct((row_count, col_count) + packed.shape, jnp.float32),
            jax.ShapeDtypeStruct((row_count,) + diag_inverse.shape, jnp.float32),
        ),
        sem_pair(col_count) + sem_pair(row_count) + sem_pair(row_count),
        (packed, diag_inverse),
    )
    chain = all_chain.reshape(row_count, col_count, NSUPER, nb_rows, nb_cols)
    chain = chain.transpose(2, 0, 3, 1, 4).reshape(NSUPER, NB, NB)
    diag = all_diag.transpose(1, 0, 2, 3).reshape(NSUPER, NB, NB)

    partial = []
    owns = []
    rows = []
    totals = []
    for current in range(NSUPER):
        summed = -dot(panels[current], inverse_sep, 1, 0)
        for earlier in range(current):
            summed = summed - dot(chain[pair_index(current, earlier)], partial[earlier], 0, 0)
        partial.append(summed)
        own, full = communicating(
            functools.partial(row_sum_kernel, row_count, ratio_cols),
            1 + current,
            (
                jax.ShapeDtypeStruct((nb_rows, col_cells), jnp.float32),
                jax.ShapeDtypeStruct((NB, col_cells), jnp.float32),
            ),
            [pltpu.VMEM((row_count, nb_rows, col_cells), jnp.float32)]
            + sem_pair(row_count)
            + sem_pair(row_count),
            (summed,),
        )
        owns.append(own)
        rows.append(full)
        own_panel = lax.dynamic_slice_in_dim(panels[current], inner_part * col_cells, col_cells, 1)
        for earlier in range(current + 1):
            totals.append(dot(rows[earlier], own_panel, 1, 1))
    part = jnp.concatenate(totals)
    total = communicating(
        functools.partial(total_kernel, row_count, col_count, ratio_cols),
        1 + NSUPER,
        jax.ShapeDtypeStruct(part.shape, jnp.float32),
        [pltpu.VMEM((col_count, part.shape[0] // col_count, NB), jnp.float32)]
        + sem_pair(col_count)
        + sem_pair(row_count)
        + sem_pair(col_count)
        + sem_pair(col_count),
        (part,),
    )
    state = pl.pallas_call(
        finish_kernel,
        out_shape=jax.ShapeDtypeStruct((NSUPER, NB, NSUPER * NB), jnp.float32),
        in_specs=[VMEM] * 3,
        out_specs=VMEM,
        compiler_params=pltpu.CompilerParams(vmem_limit_bytes=VMEM_BYTES),
    )(total, chain, diag)
    state = lax.dynamic_slice_in_dim(state, row_place * nb_rows, nb_rows, 1)
    return jnp.stack(owns), state


def solution(mesh):
    in_specs = (
        P("row", "col"),
        P(None, "row", "col"),
        P(None, "row", "col"),
        P(None, "row", None),
        P(),
    )
    out_specs = (P(None, "row", "col"), P(None, "row", None))
    return jax.shard_map(
        per_device, mesh=mesh, in_specs=in_specs, out_specs=out_specs, check_vma=False
    )
```
